32 devices in a mesh: alpha: 8 (over z, core), beta: 4 (over y, x).
Axes of the slice: x: 2, y: 2, z: 4, core: 2. Of those that a mesh axis runs over, the one named last changes fastest.
Arguments:
- ci_vector: float32 [1024, 24576], P('alpha', 'beta'), may hold values from -6 to 6
- patterns: float32 [16, 64, 64], replicated, may hold values from -0.7 to 2
- alpha_links: int32 [16, 8], replicated, may hold values from 0 to 15
- alpha_kinds: int32 [16, 8], replicated, may hold values from 0 to 15
- alpha_coefs: float32 [16, 8], replicated, may hold values from -1 to 1
- beta_links: int32 [384, 2], replicated, may hold values from 0 to 383
- beta_kinds: int32 [384, 2], replicated, may hold values from 0 to 15
- beta_coefs: float32 [384, 2], replicated, may hold values from -1 to 1
Outputs:
- sigma: float32 [1024, 24576], P('alpha', 'beta')
The draws below stay inside these ranges and needn't reach their ends.
All inputs are finite; a program needn't handle non-finite values.
Results may differ from the reference program's by a relative error of at most 0.0001.
Values sent between devices are 32-bit elements; how exact they have to be, the bound alone decides.
No kernel may reach another device: no remote copies, remote signals or barrier semaphores. Data moves between devices by JAX's collectives and lax.ppermute only.
A program may use at most 192 MiB of HBM per device.

```python
import jax
import jax.numpy as jnp
from jax import lax

BLK = 64
NPAT = 16
KA = 8
KB = 2
NB = 24576
NAB = 16
NA = 1024
NBB = 384


def draw_patterns(key, part):
    key = jax.random.fold_in(key, 7)
    key_diag, key_off = jax.random.split(key, 2)
    diagonal = jax.random.uniform(key_diag, (NPAT, BLK), jnp.float32, 1.0, 2.0)
    off_diag = 0.12 * jax.random.normal(key_off, (NPAT, BLK, BLK), jnp.float32)
    off_diag = jnp.clip(off_diag, -0.7, 0.7)
    identity = jnp.eye(BLK, dtype=jnp.float32)
    return off_diag * (1.0 - identity) + identity * diagonal[:, :, None]


def with_ends(entries, stream_key, low, top_value):
    dims = entries.shape
    place = [jax.random.randint(jax.random.fold_in(stream_key, axis), (), 0, dims[axis]) for axis in range(len(dims))]
    entries = entries.at[tuple(place)].set(low)
    longest = dims.index(max(dims))
    place[longest] = (place[longest] + 1) % dims[longest]
    return entries.at[tuple(place)].set(top_value)


def shard_levels(stream_key, shape, cuts, low, largest):
    gain = 1.0
    for axis_at, parts in cuts:
        steps = jax.random.uniform(jax.random.fold_in(jax.random.fold_in(stream_key, 6), axis_at), (parts,), jnp.float32, low / len(cuts), largest / len(cuts))
        gain = gain * jnp.repeat(jnp.exp(steps), shape[axis_at] // parts).reshape((-1,) + (1,) * (len(shape) - 1 - axis_at))
    return gain


def normal_values(stream_key, dims, scale, bound, cuts=(), held_as=jnp.bfloat16):
    factor_of = shard_levels(stream_key, dims, cuts, -0.22, 0.18) if cuts else 1.0
    array = jax.random.normal(stream_key, dims, jnp.float32) * scale * factor_of
    return jnp.minimum(jnp.maximum(array, -bound), bound).astype(held_as)


def setup_inputs(seed: int = 0) -> dict:
    seeds = jax.random.split(jax.random.key(seed), 9)
    return {
        "ci_vector": normal_values(seeds[0], (NA, NB), 1.0, 6.0, ((0, 8), (1, 4)), jnp.float32),
        "patterns": draw_patterns(jax.random.fold_in(seeds[8], 71), 0),
        "alpha_links": with_ends(jax.random.randint(seeds[2], (NAB, KA), 0, NAB), jax.random.fold_in(seeds[2], 1), 0, NAB - 1).astype(jnp.int32),
        "alpha_kinds": with_ends(jax.random.randint(seeds[3], (NAB, KA), 0, NPAT), jax.random.fold_in(seeds[3], 1), 0, NPAT - 1).astype(jnp.int32),
        "alpha_coefs": jnp.clip(jax.random.uniform(seeds[4], (NAB, KA), jnp.float32, -1.0, 1.0), -1.0, 1.0),
        "beta_links": with_ends(jax.random.randint(seeds[5], (NBB, KB), 0, NBB), jax.random.fold_in(seeds[5], 1), 0, NBB - 1).astype(jnp.int32),
        "beta_kinds": with_ends(jax.random.randint(seeds[6], (NBB, KB), 0, NPAT), jax.random.fold_in(seeds[6], 1), 0, NPAT - 1).astype(jnp.int32),
        "beta_coefs": jnp.clip(jax.random.uniform(seeds[7], (NBB, KB), jnp.float32, -1.0, 1.0), -1.0, 1.0),
    }


def alpha_term(ci_vector, patterns, links, kinds, coefs):
    block_count = links.shape[0]
    blocks = ci_vector.reshape(block_count, BLK, ci_vector.shape[1])
    running = jnp.zeros(blocks.shape, jnp.float32)
    for slot_index in range(links.shape[1]):
        matrices = patterns[kinds[:, slot_index]] * coefs[:, slot_index][:, None, None]
        gathered = blocks[links[:, slot_index]]
        running = running + jnp.einsum("ipq,iqb->ipb", matrices, gathered, precision=lax.Precision.HIGHEST)
    return running.reshape(ci_vector.shape)


def beta_term(row_data, patterns, links, kinds, coefs):
    block_count = links.shape[0]
    strided = row_data.reshape(row_data.shape[0], block_count, BLK)
    running = jnp.zeros(strided.shape, jnp.float32)
    for slot_index in range(links.shape[1]):
        matrices = patterns[kinds[:, slot_index]] * coefs[:, slot_index][:, None, None]
        gathered = strided[:, links[:, slot_index], :]
        running = running + jnp.einsum("ajq,jqp->ajp", gathered, matrices, precision=lax.Precision.HIGHEST)
    return running.reshape(row_data.shape)


def reference(ci_vector, patterns, alpha_links, alpha_kinds, alpha_coefs, beta_links, beta_kinds, beta_coefs):
    alpha_part = alpha_term(ci_vector, patterns, alpha_links, alpha_kinds, alpha_coefs)
    beta_part = beta_term(ci_vector, patterns, beta_links, beta_kinds, beta_coefs)
    return alpha_part + beta_part
```

```python
import functools

import jax
import jax.numpy as jnp
from jax import lax
from jax.experimental import pallas as pl
from jax.experimental.pallas import tpu as pltpu
from jax.sharding import PartitionSpec as P

BLK = 64
LANES = 128
CHUNKS = 2


def split(value):
    high = value.astype(jnp.bfloat16)
    low = (value - high.astype(jnp.float32)).astype(jnp.bfloat16)
    return high, low


def dot3(left, right):
    dot = functools.partial(jnp.dot, preferred_element_type=jnp.float32)
    return dot(left[0], right[0]) + (dot(left[0], right[1]) + dot(left[1], right[0]))


def alpha_kernel(count, matrix_ref, *refs):
    piece_refs = refs[:count]
    own_ref, send_ref, matrix_high, matrix_low, piece_high, piece_low = refs[count:]

    @pl.when(pl.program_id(0) == 0)
    def _():
        matrix_high[...], matrix_low[...] = split(matrix_ref[...])

    rows = own_ref.shape[0]
    for index, piece_ref in enumerate(piece_refs):
        place = pl.ds(index * rows, rows)
        piece_high[place, :], piece_low[place, :] = split(piece_ref[...])
    product = dot3(
        (matrix_high[...], matrix_low[...]), (piece_high[...], piece_low[...])
    )
    own_ref[...] = product[:rows]
    send_ref[...] = product[rows:]


def alpha_products(matrix, whole, pieces, start, width):
    rows = whole[0].shape[0]
    tile = width
    while tile > 768:
        tile //= 2
    count = len(whole) + len(pieces)
    depth = count * rows
    first = start // tile
    out = jax.ShapeDtypeStruct((rows, width), jnp.float32)
    return pl.pallas_call(
        functools.partial(alpha_kernel, count),
        grid=(width // tile,),
        in_specs=[pl.BlockSpec((2 * rows, depth), lambda i: (0, 0))]
        + [pl.BlockSpec((rows, tile), lambda i: (0, first + i))] * len(whole)
        + [pl.BlockSpec((rows, tile), lambda i: (0, i))] * len(pieces),
        out_specs=[pl.BlockSpec((rows, tile), lambda i: (0, i))] * 2,
        out_shape=[out, out],
        scratch_shapes=[pltpu.VMEM((2 * rows, depth), jnp.bfloat16)] * 2
        + [pltpu.VMEM((depth, tile), jnp.bfloat16)] * 2,
        compiler_params=pltpu.CompilerParams(vmem_limit_bytes=40 * 2**20),
        cost_estimate=pl.CostEstimate(
            flops=12 * rows * depth * width,
            bytes_accessed=4 * (depth + 2 * rows) * width,
            transcendentals=0,
        ),
    )(matrix, *whole, *pieces)


def coupling_matrix(patterns, links, kinds, coefs, target_blocks, source_blocks):
    links, kinds, coefs = links[target_blocks], kinds[target_blocks], coefs[target_blocks]
    matrices = patterns[kinds] * coefs[:, :, None, None]
    matches = (links[:, :, None] == source_blocks).astype(jnp.float32)
    coupling = jnp.einsum("osk,ospq->opkq", matches, matrices, precision=lax.Precision.HIGHEST)
    return coupling.reshape(target_blocks.shape[0] * BLK, source_blocks.shape[0] * BLK)


def beta_kernel(
    layout, me_ref, slot_ref, tile_ref, half_ref, kind_ref, coef_ref, pattern_ref, *refs
):
    parts = refs[: len(layout)]
    out_ref, data, pattern_high, pattern_low, sems = refs[len(layout) :]
    copies = []
    for index, ((flip, row, count), part) in enumerate(zip(layout, parts)):
        slot = lax.bitwise_xor(me_ref[0], flip)
        copies.append(
            pltpu.make_async_copy(part, data.at[slot, pl.ds(row, count)], sems.at[index])
        )
    for copy in copies:
        copy.start()
    pattern_high[...], pattern_low[...] = split(pattern_ref[...])
    for copy in copies:
        copy.wait()
    rows = out_ref.shape[0]
    lower = lax.broadcasted_iota(jnp.int32, (rows, LANES), 1) < BLK

    def block(item, side):
        lanes = pl.ds(pl.multiple_of(tile_ref[item] * LANES, LANES), LANES)
        value = data[slot_ref[item], :, lanes] * coef_ref[item]
        return pltpu.roll(value, BLK * lax.bitwise_xor(half_ref[item], side), 1)

    def pair(index, carry):
        first = index * 4
        left, right = [], []
        for side in (0, 1):
            item = first + 2 * side
            left.append(split(jnp.where(lower, block(item, 0), block(item + 1, 1))))
            for slot in (0, 1):
                kind = kind_ref[item + slot] * 2 + side
                right.append((pattern_high[kind], pattern_low[kind]))
        left = [jnp.concatenate([part[half] for part in left], 1) for half in (0, 1)]
        right = [jnp.concatenate([part[half] for part in right], 0) for half in (0, 1)]
        out_ref[:, pl.ds(pl.multiple_of(index * LANES, LANES), LANES)] = dot3(left, right)
        return carry

    lax.fori_loop(0, out_ref.shape[1] // LANES, pair, 0, unroll=2)


def beta_term(me, device_count, layout, parts, patterns, links, kinds, coefs, shape):
    rows, cols = shape
    own_count = cols // BLK
    own = [
        lax.dynamic_slice_in_dim(array, me * own_count, own_count, 0).reshape(-1)
        for array in (links, kinds, coefs)
    ]
    owner, place = own[0] // own_count, own[0] % own_count
    zeros = jnp.zeros_like(patterns)
    sides = jnp.stack(
        [jnp.concatenate([patterns, zeros], 2), jnp.concatenate([zeros, patterns], 2)], 1
    ).reshape(-1, BLK, LANES)
    smem = pl.BlockSpec(memory_space=pltpu.SMEM)
    vmem = pl.BlockSpec(memory_space=pltpu.VMEM)
    return pl.pallas_call(
        functools.partial(beta_kernel, layout),
        in_specs=[smem] * 6 + [vmem] + [pl.BlockSpec(memory_space=pl.ANY)] * len(parts),
        out_specs=vmem,
        out_shape=jax.ShapeDtypeStruct(shape, jnp.float32),
        scratch_shapes=[
            pltpu.VMEM((device_count, rows, cols), jnp.float32),
            pltpu.VMEM(sides.shape, jnp.bfloat16),
            pltpu.VMEM(sides.shape, jnp.bfloat16),
            pltpu.SemaphoreType.DMA((len(parts),)),
        ],
        compiler_params=pltpu.CompilerParams(vmem_limit_bytes=40 * 2**20),
        cost_estimate=pl.CostEstimate(
            flops=12 * rows * cols * 4 * BLK,
            bytes_accessed=4 * rows * cols * (device_count + 1),
            transcendentals=0,
        ),
    )(me.reshape(1), owner, place // 2, place % 2, own[1], own[2], sides, *parts)


def on_device(
    alpha_devices,
    beta_devices,
    ci_vector,
    patterns,
    alpha_links,
    alpha_kinds,
    alpha_coefs,
    beta_links,
    beta_kinds,
    beta_coefs,
):
    rows, cols = ci_vector.shape
    layers = alpha_devices // 2
    width = cols // (2 * CHUNKS)
    me = lax.axis_index("alpha")
    me_beta = lax.axis_index("beta")

    def over_alpha(value, flip):
        return lax.ppermute(value, "alpha", [(i, i ^ flip) for i in range(alpha_devices)])

    def over_beta(value, flip):
        return lax.ppermute(value, "beta", [(i, i ^ flip) for i in range(beta_devices)])

    plans = [
        ([2 * m for m in range(1, layers // 2)], layers),
        ([4 * m for m in range(1, layers // 2)], 2),
    ]
    peer = over_alpha(ci_vector, 1)
    arrived = {}
    for chunk in range(CHUNKS):
        for kind, (members, _) in enumerate(plans):
            start = (kind * CHUNKS + chunk) * width
            piece = ci_vector[:, start : start + width]
            arrived[kind, chunk] = [over_alpha(piece, flip) for flip in members]

    gathered = {0: ci_vector}
    layout, parts = [(0, 0, rows)], [ci_vector]
    for flip in range(1, beta_devices):
        low = flip & -flip
        if low == flip:
            gathered[flip] = over_beta(ci_vector, flip)
            layout.append((flip, 0, rows))
            parts.append(gathered[flip])
    for flip in range(1, beta_devices):
        low = flip & -flip
        if low != flip:
            top = over_beta(gathered[flip ^ low][: rows // 2], low)
            bottom = over_beta(gathered[low][rows // 2 :], flip ^ low)
            gathered[flip] = jnp.concatenate([top, bottom], 0)
            layout += [(flip, 0, rows // 2), (flip, rows // 2, rows // 2)]
            parts += [top, bottom]

    blocks = rows // BLK
    inner = jnp.arange(blocks, dtype=jnp.int32)
    sums = {}
    for kind, (members, partner) in enumerate(plans):
        sources = [0, 1] + [flip ^ core for flip in members for core in (0, 1)]
        targets = jnp.concatenate([(me ^ flip) * blocks + inner for flip in (0, partner)])
        source_blocks = jnp.concatenate([(me ^ flip) * blocks + inner for flip in sources])
        matrix = coupling_matrix(
            patterns, alpha_links, alpha_kinds, alpha_coefs, targets, source_blocks
        )
        for chunk in range(CHUNKS):
            pieces = []
            for piece in arrived[kind, chunk]:
                pieces += [piece, over_alpha(piece, 1)]
            start = (kind * CHUNKS + chunk) * width
            own, send = alpha_products(matrix, [ci_vector, peer], pieces, start, width)
            sums[kind, chunk] = own, over_alpha(send, partner)

    beta_part = beta_term(
        me_beta,
        beta_devices,
        tuple(layout),
        parts,
        patterns,
        beta_links,
        beta_kinds,
        beta_coefs,
        (rows, cols),
    )
    order = [sums[kind, chunk] for kind in (0, 1) for chunk in range(CHUNKS)]
    own = jnp.concatenate([own for own, _ in order], 1)
    other = jnp.concatenate([other for _, other in order], 1)
    return (own + beta_part) + other


def solution(mesh):
    return jax.shard_map(
        functools.partial(on_device, mesh.shape["alpha"], mesh.shape["beta"]),
        mesh=mesh,
        in_specs=(P("alpha", "beta"), P(), P(), P(), P(), P(), P(), P()),
        out_specs=P("alpha", "beta"),
        check_vma=False,
    )
```

```python
import functools
import math

import jax
import jax.numpy as jnp
from jax import lax
from jax.experimental import pallas as pl
from jax.experimental.pallas import tpu as pltpu
from jax.sharding import PartitionSpec as P

BLK = 64
LANES = 128


def split(value):
    high = value.astype(jnp.bfloat16)
    low = (value - high.astype(jnp.float32)).astype(jnp.bfloat16)
    return high, low


def dot3(left, right):
    dot = functools.partial(jnp.dot, preferred_element_type=jnp.float32)
    return dot(left[0], right[0]) + (dot(left[0], right[1]) + dot(left[1], right[0]))


def matrix_kernel(weight_ref, side_ref, high_ref, low_ref):
    plans, height, depth = high_ref.shape
    across, down = depth // LANES, height // BLK
    kinds = side_ref.shape[0] // 2

    def pair(index, carry):
        column = lax.rem(index, across)
        line = lax.rem(lax.div(index, across), down)
        plan = lax.div(index, across * down)
        first = index * 2 * kinds
        total = jnp.zeros((BLK, LANES), jnp.float32)
        for side in (0, 1):
            for kind in range(kinds):
                weight = weight_ref[first + side * kinds + kind]
                total = total + weight * side_ref[2 * kind + side]
        high, low = split(total)
        place = (
            plan,
            pl.ds(pl.multiple_of(line * BLK, BLK), BLK),
            pl.ds(pl.multiple_of(column * LANES, LANES), LANES),
        )
        high_ref[place] = high
        low_ref[place] = low
        return carry

    lax.fori_loop(0, plans * across * down, pair, 0)


def coupling_matrices(sides, links, kinds, coefs, targets, sources):
    kind_count = sides.shape[0] // 2
    owner = lax.broadcasted_iota(jnp.int32, links.shape, 0).reshape(-1)
    links, kinds, coefs = links.reshape(-1), kinds.reshape(-1), coefs.reshape(-1)
    at_target = jnp.where(owner == targets[..., None], coefs, 0.0)
    at_source = (links == sources[..., None]).astype(jnp.float32)
    at_kind = kinds == jnp.arange(kind_count, dtype=jnp.int32)[:, None]
    weights = jnp.sum(
        jnp.where(
            at_kind, at_target[:, :, None, None, :] * at_source[:, None, :, None, :], 0.0
        ),
        -1,
    )
    shape = (targets.shape[0], targets.shape[1] * BLK, sources.shape[1] * BLK)
    vmem = pl.BlockSpec(memory_space=pltpu.VMEM)
    return pl.pallas_call(
        matrix_kernel,
        in_specs=[pl.BlockSpec(memory_space=pltpu.SMEM), vmem],
        out_specs=[vmem, vmem],
        out_shape=[jax.ShapeDtypeStruct(shape, jnp.bfloat16)] * 2,
        compiler_params=pltpu.CompilerParams(vmem_limit_bytes=16 * 2**20),
        cost_estimate=pl.CostEstimate(
            flops=2 * kind_count * shape[0] * shape[1] * shape[2],
            bytes_accessed=4 * sides.size,
            transcendentals=0,
        ),
    )(weights.reshape(-1), sides)


def alpha_kernel(count, high_ref, low_ref, *refs):
    piece_refs = refs[:count]
    own_ref, send_ref, piece_high, piece_low = refs[count:]
    rows = own_ref.shape[0]
    for index, piece_ref in enumerate(piece_refs):
        place = pl.ds(index * rows, rows)
        piece_high[place, :], piece_low[place, :] = split(piece_ref[...])
    product = dot3((high_ref[0], low_ref[0]), (piece_high[...], piece_low[...]))
    own_ref[...] = product[:rows]
    send_ref[...] = product[rows:]


def alpha_products(kind, matrices, whole, pieces, start, width):
    rows = whole[0].shape[0]
    tile = math.gcd(math.gcd(start, width), 1024)
    count = len(whole) + len(pieces)
    depth = count * rows
    first = start // tile
    out = jax.ShapeDtypeStruct((rows, width), jnp.float32)
    return pl.pallas_call(
        functools.partial(alpha_kernel, count),
        grid=(width // tile,),
        in_specs=[pl.BlockSpec((1, 2 * rows, depth), lambda i: (kind, 0, 0))] * 2
        + [pl.BlockSpec((rows, tile), lambda i: (0, first + i))] * len(whole)
        + [pl.BlockSpec((rows, tile), lambda i: (0, i))] * len(pieces),
        out_specs=[pl.BlockSpec((rows, tile), lambda i: (0, i))] * 2,
        out_shape=[out, out],
        scratch_shapes=[pltpu.VMEM((depth, tile), jnp.bfloat16)] * 2,
        compiler_params=pltpu.CompilerParams(vmem_limit_bytes=40 * 2**20),
        cost_estimate=pl.CostEstimate(
            flops=12 * rows * depth * width,
            bytes_accessed=4 * (depth + 2 * rows) * width,
            transcendentals=0,
        ),
    )(*matrices, *whole, *pieces)


def add_kernel(starts, total_ref, *refs):
    count = len(starts)
    other_refs, out_ref, held, sums, sems = refs[:count], *refs[count:]
    width = sums.shape[2]
    loads, stores = [], []
    for index, start in enumerate(starts):
        place = pl.ds(start, width)
        loads.append(
            [
                pltpu.make_async_copy(other_refs[index], held.at[index], sems.at[3 * index]),
                pltpu.make_async_copy(
                    total_ref.at[:, place], sums.at[index], sems.at[3 * index + 1]
                ),
            ]
        )
        stores.append(
            pltpu.make_async_copy(
                sums.at[index], out_ref.at[:, place], sems.at[3 * index + 2]
            )
        )
    for pair in loads:
        for copy in pair:
            copy.start()
    for index in range(count):
        for copy in loads[index]:
            copy.wait()
        sums[index] = sums[index] + held[index]
        stores[index].start()
    for copy in stores:
        copy.wait()


def add_at(total, others, starts):
    rows, width = others[0].shape
    count = len(starts)
    anywhere = pl.BlockSpec(memory_space=pl.ANY)
    return pl.pallas_call(
        functools.partial(add_kernel, starts),
        in_specs=[anywhere] * (1 + count),
        out_specs=anywhere,
        out_shape=jax.ShapeDtypeStruct(total.shape, jnp.float32),
        scratch_shapes=[pltpu.VMEM((count, rows, width), jnp.float32)] * 2
        + [pltpu.SemaphoreType.DMA((3 * count,))],
        compiler_params=pltpu.CompilerParams(vmem_limit_bytes=48 * 2**20),
        input_output_aliases={0: 0},
    )(total, *others)


def after(value, *others):
    return lax.optimization_barrier((value, *others))[0]


def beta_kernel(
    layout, me_ref, slot_ref, tile_ref, half_ref, kind_ref, coef_ref, pattern_ref, *refs
):
    parts = refs[: len(layout)]
    out_ref, data, pattern_high, pattern_low, sems = refs[len(layout) :]
    copies = []
    for index, ((flip, row, count), part) in enumerate(zip(layout, parts)):
        slot = lax.bitwise_xor(me_ref[0], flip)
        copies.append(
            pltpu.make_async_copy(part, data.at[slot, pl.ds(row, count)], sems.at[index])
        )
    for copy in copies:
        copy.start()
    pattern_high[...], pattern_low[...] = split(pattern_ref[...])
    for copy in copies:
        copy.wait()
    rows = out_ref.shape[0]
    lower = lax.broadcasted_iota(jnp.int32, (rows, LANES), 1) < BLK

    def block(item, side):
        lanes = pl.ds(pl.multiple_of(tile_ref[item] * LANES, LANES), LANES)
        value = data[slot_ref[item], :, lanes] * coef_ref[item]
        return pltpu.roll(value, BLK * lax.bitwise_xor(half_ref[item], side), 1)

    def pair(index, carry):
        first = index * 4
        left, right = [], []
        for side in (0, 1):
            item = first + 2 * side
            left.append(split(jnp.where(lower, block(item, 0), block(item + 1, 1))))
            for slot in (0, 1):
                kind = kind_ref[item + slot] * 2 + side
                right.append((pattern_high[kind], pattern_low[kind]))
        left = [jnp.concatenate([part[half] for part in left], 1) for half in (0, 1)]
        right = [jnp.concatenate([part[half] for part in right], 0) for half in (0, 1)]
        out_ref[:, pl.ds(pl.multiple_of(index * LANES, LANES), LANES)] = dot3(left, right)
        return carry

    lax.fori_loop(0, out_ref.shape[1] // LANES, pair, 0, unroll=2)


def padded_patterns(patterns):
    zeros = jnp.zeros_like(patterns)
    left = jnp.concatenate([patterns, zeros], 2)
    right = jnp.concatenate([zeros, patterns], 2)
    return jnp.stack([left, right], 1).reshape(-1, BLK, LANES)


def beta_tables(me, own_count, links, kinds, coefs):
    links, kinds, coefs = [
        lax.dynamic_slice_in_dim(array, me * own_count, own_count, 0).reshape(-1)
        for array in (links, kinds, coefs)
    ]
    owner, place = lax.div(links, own_count), lax.rem(links, own_count)
    return owner, lax.div(place, 2), lax.rem(place, 2), kinds, coefs


def beta_term(me, device_count, layout, parts, tables, sides, shape):
    rows, cols = shape
    smem = pl.BlockSpec(memory_space=pltpu.SMEM)
    vmem = pl.BlockSpec(memory_space=pltpu.VMEM)
    return pl.pallas_call(
        functools.partial(beta_kernel, layout),
        in_specs=[smem] * 6 + [vmem] + [pl.BlockSpec(memory_space=pl.ANY)] * len(parts),
        out_specs=vmem,
        out_shape=jax.ShapeDtypeStruct(shape, jnp.float32),
        scratch_shapes=[
            pltpu.VMEM((device_count, rows, cols), jnp.float32),
            pltpu.VMEM(sides.shape, jnp.bfloat16),
            pltpu.VMEM(sides.shape, jnp.bfloat16),
            pltpu.SemaphoreType.DMA((len(parts),)),
        ],
        compiler_params=pltpu.CompilerParams(vmem_limit_bytes=40 * 2**20),
        cost_estimate=pl.CostEstimate(
            flops=12 * rows * cols * 4 * BLK,
            bytes_accessed=4 * rows * cols * (device_count + 1),
            transcendentals=0,
        ),
    )(me.reshape(1), *tables, sides, *parts)


def on_device(
    alpha_devices,
    beta_devices,
    ci_vector,
    patterns,
    alpha_links,
    alpha_kinds,
    alpha_coefs,
    beta_links,
    beta_kinds,
    beta_coefs,
):
    rows, cols = ci_vector.shape
    layers = alpha_devices // 2
    me = lax.axis_index("alpha")
    me_beta = lax.axis_index("beta")

    def over_alpha(value, flip):
        return lax.ppermute(value, "alpha", [(i, i ^ flip) for i in range(alpha_devices)])

    def over_beta(value, flip):
        return lax.ppermute(value, "beta", [(i, i ^ flip) for i in range(beta_devices)])

    plans = [
        ([2 * m for m in range(1, layers // 2)], layers),
        ([4 * m for m in range(1, layers // 2)], 2),
    ]
    width = cols // 4

    def start_of(kind, chunk):
        return (2 * kind + chunk) * width

    peer = over_alpha(ci_vector, 1)
    blocks = rows // BLK
    inner = jnp.arange(blocks, dtype=jnp.int32)
    targets, sources = [], []
    for members, partner in plans:
        flips = [0, 1] + [flip ^ core for flip in members for core in (0, 1)]
        targets.append(
            jnp.concatenate([(me ^ flip) * blocks + inner for flip in (0, partner)])
        )
        sources.append(jnp.concatenate([(me ^ flip) * blocks + inner for flip in flips]))
    sides = after(padded_patterns(patterns), peer)
    matrices = coupling_matrices(
        sides, alpha_links, alpha_kinds, alpha_coefs, jnp.stack(targets), jnp.stack(sources)
    )
    tables = beta_tables(me_beta, cols // BLK, beta_links, beta_kinds, beta_coefs)

    arrived = {}
    for chunk in (0, 1):
        for kind in (1, 0):
            start = start_of(kind, chunk)
            source = after(ci_vector, *arrived[kind, 0]) if chunk else ci_vector
            piece = source[:, start : start + width]
            arrived[kind, chunk] = [over_alpha(piece, flip) for flip in plans[kind][0]]

    def swap(chunk, *earlier):
        swapped = []
        for kind in (0, 1):
            swapped.append([])
            for piece in arrived[kind, chunk]:
                swapped[kind] += [piece, over_alpha(after(piece, *earlier), 1)]
        return swapped

    own, others = {}, {}

    def multiply(chunk, swapped):
        sends = []
        for kind, (_, partner) in enumerate(plans):
            own[kind, chunk], send = alpha_products(
                kind, matrices, [ci_vector, peer], swapped[kind], start_of(kind, chunk), width
            )
            others[kind, chunk] = over_alpha(send, partner)
            sends.append(send)
        return sends

    sends = multiply(0, swap(0, *matrices, *tables))

    whole = after(ci_vector, peer)
    gathered = {0: ci_vector}
    layout, parts = [(0, 0, rows)], [ci_vector]
    for flip in range(1, beta_devices):
        if flip & -flip == flip:
            gathered[flip] = over_beta(whole, flip)
            layout.append((flip, 0, rows))
            parts.append(gathered[flip])
    for flip in range(1, beta_devices):
        low = flip & -flip
        if low != flip:
            first = after(gathered[flip ^ low], *sends)[: rows // 2]
            second = after(gathered[low], *sends)[rows // 2 :]
            top = over_beta(first, low)
            bottom = over_beta(second, flip ^ low)
            gathered[flip] = jnp.concatenate([top, bottom], 0)
            layout += [(flip, 0, rows // 2), (flip, rows // 2, rows // 2)]
            parts += [top, bottom]

    multiply(1, swap(1, *sends))
    total = beta_term(
        me_beta, beta_devices, tuple(layout), parts, tables, sides, (rows, cols)
    )
    total = total + jnp.concatenate(
        [own[kind, chunk] for kind in (0, 1) for chunk in (0, 1)], 1
    )
    for chunk in (0, 1):
        total = add_at(
            total,
            [after(others[kind, chunk], total) for kind in (0, 1)],
            [start_of(kind, chunk) for kind in (0, 1)],
        )
    return total


def solution(mesh):
    return jax.shard_map(
        functools.partial(on_device, mesh.shape["alpha"], mesh.shape["beta"]),
        mesh=mesh,
        in_specs=(P("alpha", "beta"), P(), P(), P(), P(), P(), P(), P()),
        out_specs=P("alpha", "beta"),
        check_vma=False,
    )
```

```python
import functools
import math

import jax
import jax.numpy as jnp
from jax import lax
from jax.experimental import pallas as pl
from jax.experimental.pallas import tpu as pltpu
from jax.sharding import PartitionSpec as P

BLK = 64
LANES = 128
SPLITS = 4


def split(value):
    high = value.astype(jnp.bfloat16)
    low = (value - high.astype(jnp.float32)).astype(jnp.bfloat16)
    return high, low


def dot3(left, right):
    dot = functools.partial(jnp.dot, preferred_element_type=jnp.float32)
    return dot(left[0], right[0]) + (dot(left[0], right[1]) + dot(left[1], right[0]))


def matrix_kernel(weight_ref, side_ref, high_ref, low_ref):
    plans, height, depth = high_ref.shape
    across, down = depth // LANES, height // BLK
    kinds = side_ref.shape[0] // 2

    def pair(index, carry):
        column = lax.rem(index, across)
        line = lax.rem(lax.div(index, across), down)
        plan = lax.div(index, across * down)
        first = index * 2 * kinds
        total = jnp.zeros((BLK, LANES), jnp.float32)
        for side in (0, 1):
            for kind in range(kinds):
                weight = weight_ref[first + side * kinds + kind]
                total = total + weight * side_ref[2 * kind + side]
        high, low = split(total)
        place = (
            plan,
            pl.ds(pl.multiple_of(line * BLK, BLK), BLK),
            pl.ds(pl.multiple_of(column * LANES, LANES), LANES),
        )
        high_ref[place] = high
        low_ref[place] = low
        return carry

    lax.fori_loop(0, plans * across * down, pair, 0)


def coupling_matrices(sides, links, kinds, coefs, targets, sources):
    kind_count = sides.shape[0] // 2
    owner = lax.broadcasted_iota(jnp.int32, links.shape, 0).reshape(-1)
    links, kinds, coefs = links.reshape(-1), kinds.reshape(-1), coefs.reshape(-1)
    at_target = jnp.where(owner == targets[..., None], coefs, 0.0)
    at_source = (links == sources[..., None]).astype(jnp.float32)
    at_kind = kinds == jnp.arange(kind_count, dtype=jnp.int32)[:, None]
    weights = jnp.sum(
        jnp.where(
            at_kind, at_target[:, :, None, None, :] * at_source[:, None, :, None, :], 0.0
        ),
        -1,
    )
    shape = (targets.shape[0], targets.shape[1] * BLK, sources.shape[1] * BLK)
    vmem = pl.BlockSpec(memory_space=pltpu.VMEM)
    return pl.pallas_call(
        matrix_kernel,
        in_specs=[pl.BlockSpec(memory_space=pltpu.SMEM), vmem],
        out_specs=[vmem, vmem],
        out_shape=[jax.ShapeDtypeStruct(shape, jnp.bfloat16)] * 2,
        compiler_params=pltpu.CompilerParams(vmem_limit_bytes=16 * 2**20),
        cost_estimate=pl.CostEstimate(
            flops=2 * kind_count * shape[0] * shape[1] * shape[2],
            bytes_accessed=4 * sides.size,
            transcendentals=0,
        ),
    )(weights.reshape(-1), sides)


def alpha_kernel(count, high_ref, low_ref, *refs):
    piece_refs = refs[:count]
    own_ref, send_ref, piece_high, piece_low = refs[count:]
    rows = own_ref.shape[0]
    for index, piece_ref in enumerate(piece_refs):
        place = pl.ds(index * rows, rows)
        piece_high[place, :], piece_low[place, :] = split(piece_ref[...])
    product = dot3((high_ref[0], low_ref[0]), (piece_high[...], piece_low[...]))
    own_ref[...] = product[:rows]
    send_ref[...] = product[rows:]


def alpha_products(kind, matrices, whole, pieces, start, width):
    rows = whole[0].shape[0]
    tile = math.gcd(math.gcd(start, width), 1024)
    count = len(whole) + len(pieces)
    depth = count * rows
    first = start // tile
    out = jax.ShapeDtypeStruct((rows, width), jnp.float32)
    return pl.pallas_call(
        functools.partial(alpha_kernel, count),
        grid=(width // tile,),
        in_specs=[pl.BlockSpec((1, 2 * rows, depth), lambda i: (kind, 0, 0))] * 2
        + [pl.BlockSpec((rows, tile), lambda i: (0, first + i))] * len(whole)
        + [pl.BlockSpec((rows, tile), lambda i: (0, i))] * len(pieces),
        out_specs=[pl.BlockSpec((rows, tile), lambda i: (0, i))] * 2,
        out_shape=[out, out],
        scratch_shapes=[pltpu.VMEM((depth, tile), jnp.bfloat16)] * 2,
        compiler_params=pltpu.CompilerParams(vmem_limit_bytes=40 * 2**20),
        cost_estimate=pl.CostEstimate(
            flops=12 * rows * depth * width,
            bytes_accessed=4 * (depth + 2 * rows) * width,
            transcendentals=0,
        ),
    )(*matrices, *whole, *pieces)


def take_kernel(places, source_count, *refs):
    source_refs, (*out_refs, held, sems) = refs[:source_count], refs[source_count:]
    loads, stores = [], []
    for number, ((index, row, start), out_ref) in enumerate(zip(places, out_refs)):
        rows, width = out_ref.shape
        step = rows // SPLITS
        for part in range(SPLITS):
            place = pl.ds(part * step, step)
            loads.append(
                pltpu.make_async_copy(
                    source_refs[index].at[pl.ds(row + part * step, step), pl.ds(start, width)],
                    held.at[number, place],
                    sems.at[0, len(loads)],
                )
            )
            stores.append(
                pltpu.make_async_copy(
                    held.at[number, place], out_ref.at[place], sems.at[1, len(stores)]
                )
            )
    for load in loads:
        load.start()
    for load, store in zip(loads, stores):
        load.wait()
        store.start()
    for store in stores:
        store.wait()


def take(sources, places, shapes, limit=16):
    anywhere = pl.BlockSpec(memory_space=pl.ANY)
    return pl.pallas_call(
        functools.partial(take_kernel, tuple(places), len(sources)),
        in_specs=[anywhere] * len(sources),
        out_specs=[anywhere] * len(places),
        out_shape=[jax.ShapeDtypeStruct(shape, jnp.float32) for shape in shapes],
        scratch_shapes=[
            pltpu.VMEM((len(places), *shapes[0]), jnp.float32),
            pltpu.SemaphoreType.DMA((2, SPLITS * len(places))),
        ],
        compiler_params=pltpu.CompilerParams(vmem_limit_bytes=limit * 2**20),
        cost_estimate=pl.CostEstimate(
            flops=0, bytes_accessed=sum(8 * a * b for a, b in shapes), transcendentals=0
        ),
    )(*sources)


def add_kernel(starts, total_ref, *refs):
    count = len(starts)
    other_refs, out_ref, held, sums, sems = refs[:count], *refs[count:]
    width = sums.shape[2]
    loads, stores = [], []
    for index, start in enumerate(starts):
        place = pl.ds(start, width)
        loads.append(
            [
                pltpu.make_async_copy(other_refs[index], held.at[index], sems.at[3 * index]),
                pltpu.make_async_copy(
                    total_ref.at[:, place], sums.at[index], sems.at[3 * index + 1]
                ),
            ]
        )
        stores.append(
            pltpu.make_async_copy(
                sums.at[index], out_ref.at[:, place], sems.at[3 * index + 2]
            )
        )
    for pair in loads:
        for copy in pair:
            copy.start()
    for index in range(count):
        for copy in loads[index]:
            copy.wait()
        sums[index] = sums[index] + held[index]
        stores[index].start()
    for copy in stores:
        copy.wait()


def add_at(total, others, starts):
    rows, width = others[0].shape
    count = len(starts)
    anywhere = pl.BlockSpec(memory_space=pl.ANY)
    return pl.pallas_call(
        functools.partial(add_kernel, starts),
        in_specs=[anywhere] * (1 + count),
        out_specs=anywhere,
        out_shape=jax.ShapeDtypeStruct(total.shape, jnp.float32),
        scratch_shapes=[pltpu.VMEM((count, rows, width), jnp.float32)] * 2
        + [pltpu.SemaphoreType.DMA((3 * count,))],
        compiler_params=pltpu.CompilerParams(vmem_limit_bytes=48 * 2**20),
        input_output_aliases={0: 0},
    )(total, *others)


def after(value, *others):
    return lax.optimization_barrier((value, *others))[0]


def beta_kernel(
    layout, me_ref, slot_ref, tile_ref, half_ref, kind_ref, coef_ref, pattern_ref, *refs
):
    parts = refs[: len(layout)]
    out_ref, data, pattern_high, pattern_low, sems = refs[len(layout) :]
    copies = []
    for index, ((flip, row, count), part) in enumerate(zip(layout, parts)):
        slot = lax.bitwise_xor(me_ref[0], flip)
        copies.append(
            pltpu.make_async_copy(part, data.at[slot, pl.ds(row, count)], sems.at[index])
        )
    for copy in copies:
        copy.start()
    pattern_high[...], pattern_low[...] = split(pattern_ref[...])
    for copy in copies:
        copy.wait()
    rows = out_ref.shape[0]
    lower = lax.broadcasted_iota(jnp.int32, (rows, LANES), 1) < BLK

    def block(item, side):
        lanes = pl.ds(pl.multiple_of(tile_ref[item] * LANES, LANES), LANES)
        value = data[slot_ref[item], :, lanes] * coef_ref[item]
        return pltpu.roll(value, BLK * lax.bitwise_xor(half_ref[item], side), 1)

    def pair(index, carry):
        first = index * 4
        left, right = [], []
        for side in (0, 1):
            item = first + 2 * side
            left.append(split(jnp.where(lower, block(item, 0), block(item + 1, 1))))
            for slot in (0, 1):
                kind = kind_ref[item + slot] * 2 + side
                right.append((pattern_high[kind], pattern_low[kind]))
        left = [jnp.concatenate([part[half] for part in left], 1) for half in (0, 1)]
        right = [jnp.concatenate([part[half] for part in right], 0) for half in (0, 1)]
        out_ref[:, pl.ds(pl.multiple_of(index * LANES, LANES), LANES)] = dot3(left, right)
        return carry

    lax.fori_loop(0, out_ref.shape[1] // LANES, pair, 0, unroll=2)


def padded_patterns(patterns):
    zeros = jnp.zeros_like(patterns)
    left = jnp.concatenate([patterns, zeros], 2)
    right = jnp.concatenate([zeros, patterns], 2)
    return jnp.stack([left, right], 1).reshape(-1, BLK, LANES)


def beta_tables(me, own_count, links, kinds, coefs):
    links, kinds, coefs = [
        lax.dynamic_slice_in_dim(array, me * own_count, own_count, 0).reshape(-1)
        for array in (links, kinds, coefs)
    ]
    owner, place = lax.div(links, own_count), lax.rem(links, own_count)
    return owner, lax.div(place, 2), lax.rem(place, 2), kinds, coefs


def beta_term(me, device_count, layout, parts, tables, sides, shape):
    rows, cols = shape
    smem = pl.BlockSpec(memory_space=pltpu.SMEM)
    vmem = pl.BlockSpec(memory_space=pltpu.VMEM)
    return pl.pallas_call(
        functools.partial(beta_kernel, layout),
        in_specs=[smem] * 6 + [vmem] + [pl.BlockSpec(memory_space=pl.ANY)] * len(parts),
        out_specs=vmem,
        out_shape=jax.ShapeDtypeStruct(shape, jnp.float32),
        scratch_shapes=[
            pltpu.VMEM((device_count, rows, cols), jnp.float32),
            pltpu.VMEM(sides.shape, jnp.bfloat16),
            pltpu.VMEM(sides.shape, jnp.bfloat16),
            pltpu.SemaphoreType.DMA((len(parts),)),
        ],
        compiler_params=pltpu.CompilerParams(vmem_limit_bytes=40 * 2**20),
        cost_estimate=pl.CostEstimate(
            flops=12 * rows * cols * 4 * BLK,
            bytes_accessed=4 * rows * cols * (device_count + 1),
            transcendentals=0,
        ),
    )(me.reshape(1), *tables, sides, *parts)


def on_device(
    alpha_devices,
    beta_devices,
    ci_vector,
    patterns,
    alpha_links,
    alpha_kinds,
    alpha_coefs,
    beta_links,
    beta_kinds,
    beta_coefs,
):
    rows, cols = ci_vector.shape
    layers = alpha_devices // 2
    me = lax.axis_index("alpha")
    me_beta = lax.axis_index("beta")

    def over_alpha(value, flip):
        return lax.ppermute(value, "alpha", [(i, i ^ flip) for i in range(alpha_devices)])

    def over_beta(value, flip):
        return lax.ppermute(value, "beta", [(i, i ^ flip) for i in range(beta_devices)])

    plans = [
        ([2 * m for m in range(1, layers // 2)], layers),
        ([4 * m for m in range(1, layers // 2)], 2),
    ]
    width = cols // 4

    def start_of(kind, chunk):
        return (2 * kind + chunk) * width

    peer = over_alpha(ci_vector, 1)
    blocks = rows // BLK
    inner = jnp.arange(blocks, dtype=jnp.int32)
    targets, sources = [], []
    for members, partner in plans:
        flips = [0, 1] + [flip ^ core for flip in members for core in (0, 1)]
        targets.append(
            jnp.concatenate([(me ^ flip) * blocks + inner for flip in (0, partner)])
        )
        sources.append(jnp.concatenate([(me ^ flip) * blocks + inner for flip in flips]))
    sides = after(padded_patterns(patterns), peer)
    matrices = coupling_matrices(
        sides, alpha_links, alpha_kinds, alpha_coefs, jnp.stack(targets), jnp.stack(sources)
    )
    tables = beta_tables(me_beta, cols // BLK, beta_links, beta_kinds, beta_coefs)

    arrived = {}
    pieces = take(
        [ci_vector], [(0, 0, start_of(kind, 0)) for kind in (1, 0)], [(rows, width)] * 2, 56
    )
    pieces += take(
        [after(ci_vector, *matrices)],
        [(0, 0, start_of(kind, 1)) for kind in (1, 0)],
        [(rows, width)] * 2,
    )
    for chunk in (0, 1):
        for kind in (1, 0):
            piece = pieces[2 * chunk + 1 - kind]
            arrived[kind, chunk] = [over_alpha(piece, flip) for flip in plans[kind][0]]

    def swap(chunk, *earlier):
        swapped = []
        for kind in (0, 1):
            swapped.append([])
            for piece in arrived[kind, chunk]:
                swapped[kind] += [piece, over_alpha(after(piece, *earlier), 1)]
        return swapped

    own, others = {}, {}

    def multiply(chunk, swapped):
        sends = []
        for kind, (_, partner) in enumerate(plans):
            own[kind, chunk], send = alpha_products(
                kind, matrices, [ci_vector, peer], swapped[kind], start_of(kind, chunk), width
            )
            others[kind, chunk] = over_alpha(send, partner)
            sends.append(send)
        return sends

    sends = multiply(0, swap(0, *matrices, *tables, *pieces[2:]))

    whole = after(ci_vector, peer)
    gathered = {0: ci_vector}
    layout, parts = [(0, 0, rows)], [ci_vector]
    for flip in range(1, beta_devices):
        if flip & -flip == flip:
            gathered[flip] = over_beta(whole, flip)
            layout.append((flip, 0, rows))
            parts.append(gathered[flip])
    for flip in range(1, beta_devices):
        low = flip & -flip
        if low != flip:
            first, second = take(
                [after(gathered[flip ^ low], *sends), gathered[low]],
                [(0, 0, 0), (1, rows // 2, 0)],
                [(rows // 2, cols)] * 2,
            )
            top = over_beta(first, low)
            bottom = over_beta(second, flip ^ low)
            gathered[flip] = jnp.concatenate([top, bottom], 0)
            layout += [(flip, 0, rows // 2), (flip, rows // 2, rows // 2)]
            parts += [top, bottom]

    multiply(1, swap(1, *sends))
    total = beta_term(
        me_beta, beta_devices, tuple(layout), parts, tables, sides, (rows, cols)
    )
    total = total + jnp.concatenate(
        [own[kind, chunk] for kind in (0, 1) for chunk in (0, 1)], 1
    )
    for chunk in (0, 1):
        total = add_at(
            total,
            [after(others[kind, chunk], total) for kind in (0, 1)],
            [start_of(kind, chunk) for kind in (0, 1)],
        )
    return total


def solution(mesh):
    return jax.shard_map(
        functools.partial(on_device, mesh.shape["alpha"], mesh.shape["beta"]),
        mesh=mesh,
        in_specs=(P("alpha", "beta"), P(), P(), P(), P(), P(), P(), P()),
        out_specs=P("alpha", "beta"),
        check_vma=False,
    )
```

```python
import functools
import math

import jax
import jax.numpy as jnp
from jax import lax
from jax.experimental import pallas as pl
from jax.experimental.pallas import tpu as pltpu
from jax.sharding import PartitionSpec as P

BLK = 64
LANES = 128
SPLITS = 4


def split(value):
    high = value.astype(jnp.bfloat16)
    low = (value - high.astype(jnp.float32)).astype(jnp.bfloat16)
    return high, low


def dot3(left, right):
    dot = functools.partial(jnp.dot, preferred_element_type=jnp.float32)
    return dot(left[0], right[0]) + (dot(left[0], right[1]) + dot(left[1], right[0]))


def matrix_kernel(weight_ref, side_ref, high_ref, low_ref):
    plans, height, depth = high_ref.shape
    across, down = depth // LANES, height // BLK
    kinds = side_ref.shape[0] // 2

    def pair(index, carry):
        column = lax.rem(index, across)
        line = lax.rem(lax.div(index, across), down)
        plan = lax.div(index, across * down)
        first = index * 2 * kinds
        total = jnp.zeros((BLK, LANES), jnp.float32)
        for side in (0, 1):
            for kind in range(kinds):
                weight = weight_ref[first + side * kinds + kind]
                total = total + weight * side_ref[2 * kind + side]
        high, low = split(total)
        place = (
            plan,
            pl.ds(pl.multiple_of(line * BLK, BLK), BLK),
            pl.ds(pl.multiple_of(column * LANES, LANES), LANES),
        )
        high_ref[place] = high
        low_ref[place] = low
        return carry

    lax.fori_loop(0, plans * across * down, pair, 0)


def coupling_matrices(sides, links, kinds, coefs, targets, sources):
    kind_count = sides.shape[0] // 2
    owner = lax.broadcasted_iota(jnp.int32, links.shape, 0).reshape(-1)
    links, kinds, coefs = links.reshape(-1), kinds.reshape(-1), coefs.reshape(-1)
    at_target = jnp.where(owner == targets[..., None], coefs, 0.0)
    at_source = (links == sources[..., None]).astype(jnp.float32)
    at_kind = kinds == jnp.arange(kind_count, dtype=jnp.int32)[:, None]
    weights = jnp.sum(
        jnp.where(
            at_kind, at_target[:, :, None, None, :] * at_source[:, None, :, None, :], 0.0
        ),
        -1,
    )
    shape = (targets.shape[0], targets.shape[1] * BLK, sources.shape[1] * BLK)
    vmem = pl.BlockSpec(memory_space=pltpu.VMEM)
    return pl.pallas_call(
        matrix_kernel,
        in_specs=[pl.BlockSpec(memory_space=pltpu.SMEM), vmem],
        out_specs=[vmem, vmem],
        out_shape=[jax.ShapeDtypeStruct(shape, jnp.bfloat16)] * 2,
        compiler_params=pltpu.CompilerParams(vmem_limit_bytes=16 * 2**20),
        cost_estimate=pl.CostEstimate(
            flops=2 * kind_count * shape[0] * shape[1] * shape[2],
            bytes_accessed=4 * sides.size,
            transcendentals=0,
        ),
    )(weights.reshape(-1), sides)


def alpha_kernel(count, high_ref, low_ref, *refs):
    piece_refs = refs[:count]
    own_ref, send_ref, piece_high, piece_low = refs[count:]
    rows = own_ref.shape[0]
    for index, piece_ref in enumerate(piece_refs):
        place = pl.ds(index * rows, rows)
        piece_high[place, :], piece_low[place, :] = split(piece_ref[...])
    product = dot3((high_ref[0], low_ref[0]), (piece_high[...], piece_low[...]))
    own_ref[...] = product[:rows]
    send_ref[...] = product[rows:]


def alpha_products(kind, matrices, whole, pieces, start, width):
    rows = whole[0].shape[0]
    tile = math.gcd(math.gcd(start, width), 1024)
    count = len(whole) + len(pieces)
    depth = count * rows
    first = start // tile
    out = jax.ShapeDtypeStruct((rows, width), jnp.float32)
    return pl.pallas_call(
        functools.partial(alpha_kernel, count),
        grid=(width // tile,),
        in_specs=[pl.BlockSpec((1, 2 * rows, depth), lambda i: (kind, 0, 0))] * 2
        + [pl.BlockSpec((rows, tile), lambda i: (0, first + i))] * len(whole)
        + [pl.BlockSpec((rows, tile), lambda i: (0, i))] * len(pieces),
        out_specs=[pl.BlockSpec((rows, tile), lambda i: (0, i))] * 2,
        out_shape=[out, out],
        scratch_shapes=[pltpu.VMEM((depth, tile), jnp.bfloat16)] * 2,
        compiler_params=pltpu.CompilerParams(vmem_limit_bytes=40 * 2**20),
        cost_estimate=pl.CostEstimate(
            flops=12 * rows * depth * width,
            bytes_accessed=4 * (depth + 2 * rows) * width,
            transcendentals=0,
        ),
    )(*matrices, *whole, *pieces)


def take_kernel(places, source_count, *refs):
    source_refs, (*out_refs, held, sems) = refs[:source_count], refs[source_count:]
    loads, stores = [], []
    for number, ((index, row, start), out_ref) in enumerate(zip(places, out_refs)):
        rows, width = out_ref.shape
        step = rows // SPLITS
        for part in range(SPLITS):
            place = pl.ds(part * step, step)
            loads.append(
                pltpu.make_async_copy(
                    source_refs[index].at[pl.ds(row + part * step, step), pl.ds(start, width)],
                    held.at[number, place],
                    sems.at[0, len(loads)],
                )
            )
            stores.append(
                pltpu.make_async_copy(
                    held.at[number, place], out_ref.at[place], sems.at[1, len(stores)]
                )
            )
    for load in loads:
        load.start()
    for load, store in zip(loads, stores):
        load.wait()
        store.start()
    for store in stores:
        store.wait()


def take(sources, places, shapes, limit=16):
    anywhere = pl.BlockSpec(memory_space=pl.ANY)
    return pl.pallas_call(
        functools.partial(take_kernel, tuple(places), len(sources)),
        in_specs=[anywhere] * len(sources),
        out_specs=[anywhere] * len(places),
        out_shape=[jax.ShapeDtypeStruct(shape, jnp.float32) for shape in shapes],
        scratch_shapes=[
            pltpu.VMEM((len(places), *shapes[0]), jnp.float32),
            pltpu.SemaphoreType.DMA((2, SPLITS * len(places))),
        ],
        compiler_params=pltpu.CompilerParams(vmem_limit_bytes=limit * 2**20),
        cost_estimate=pl.CostEstimate(
            flops=0, bytes_accessed=sum(8 * a * b for a, b in shapes), transcendentals=0
        ),
    )(*sources)


def add_kernel(starts, total_ref, *refs):
    count = len(starts)
    other_refs, out_ref, held, sums, sems = refs[:count], *refs[count:]
    width = sums.shape[2]
    loads, stores = [], []
    for index, start in enumerate(starts):
        place = pl.ds(start, width)
        loads.append(
            [
                pltpu.make_async_copy(other_refs[index], held.at[index], sems.at[3 * index]),
                pltpu.make_async_copy(
                    total_ref.at[:, place], sums.at[index], sems.at[3 * index + 1]
                ),
            ]
        )
        stores.append(
            pltpu.make_async_copy(
                sums.at[index], out_ref.at[:, place], sems.at[3 * index + 2]
            )
        )
    for pair in loads:
        for copy in pair:
            copy.start()
    for index in range(count):
        for copy in loads[index]:
            copy.wait()
        sums[index] = sums[index] + held[index]
        stores[index].start()
    for copy in stores:
        copy.wait()


def add_at(total, others, starts):
    rows, width = others[0].shape
    count = len(starts)
    anywhere = pl.BlockSpec(memory_space=pl.ANY)
    return pl.pallas_call(
        functools.partial(add_kernel, starts),
        in_specs=[anywhere] * (1 + count),
        out_specs=anywhere,
        out_shape=jax.ShapeDtypeStruct(total.shape, jnp.float32),
        scratch_shapes=[pltpu.VMEM((count, rows, width), jnp.float32)] * 2
        + [pltpu.SemaphoreType.DMA((3 * count,))],
        compiler_params=pltpu.CompilerParams(vmem_limit_bytes=48 * 2**20),
        input_output_aliases={0: 0},
    )(total, *others)


def last_kernel(starts, *refs):
    count = len(starts)
    other_refs, base_refs = refs[1 : 1 + count], refs[1 + count : 1 + 2 * count]
    out_ref, held, sems = refs[1 + 2 * count :]
    width = held.shape[2]
    loads, stores = [], []
    for index, start in enumerate(starts):
        loads.append(
            pltpu.make_async_copy(other_refs[index], held.at[index], sems.at[2 * index])
        )
        stores.append(
            pltpu.make_async_copy(
                held.at[index], out_ref.at[:, pl.ds(start, width)], sems.at[2 * index + 1]
            )
        )
    for load in loads:
        load.start()
    for index in range(count):
        loads[index].wait()
        held[index] = held[index] + base_refs[index][...]
        stores[index].start()
    for store in stores:
        store.wait()


def add_last(total, bases, others, starts):
    rows, width = others[0].shape
    count = len(starts)
    anywhere = pl.BlockSpec(memory_space=pl.ANY)
    return pl.pallas_call(
        functools.partial(last_kernel, starts),
        in_specs=[anywhere] * (1 + count) + [pl.BlockSpec(memory_space=pltpu.VMEM)] * count,
        out_specs=anywhere,
        out_shape=jax.ShapeDtypeStruct(total.shape, jnp.float32),
        scratch_shapes=[
            pltpu.VMEM((count, rows, width), jnp.float32),
            pltpu.SemaphoreType.DMA((2 * count,)),
        ],
        compiler_params=pltpu.CompilerParams(vmem_limit_bytes=40 * 2**20),
        input_output_aliases={0: 0},
    )(total, *others, *bases)


def after(value, *others):
    return lax.optimization_barrier((value, *others))[0]


def beta_kernel(
    layout, me_ref, slot_ref, tile_ref, half_ref, kind_ref, coef_ref, pattern_ref, *refs
):
    parts = refs[: len(layout)]
    out_ref, data, pattern_high, pattern_low, sems = refs[len(layout) :]
    copies = []
    for index, ((flip, row, count), part) in enumerate(zip(layout, parts)):
        slot = lax.bitwise_xor(me_ref[0], flip)
        copies.append(
            pltpu.make_async_copy(part, data.at[slot, pl.ds(row, count)], sems.at[index])
        )
    for copy in copies:
        copy.start()
    pattern_high[...], pattern_low[...] = split(pattern_ref[...])
    for copy in copies:
        copy.wait()
    rows = out_ref.shape[0]
    lower = lax.broadcasted_iota(jnp.int32, (rows, LANES), 1) < BLK

    def block(item, side):
        lanes = pl.ds(pl.multiple_of(tile_ref[item] * LANES, LANES), LANES)
        value = data[slot_ref[item], :, lanes] * coef_ref[item]
        return pltpu.roll(value, BLK * lax.bitwise_xor(half_ref[item], side), 1)

    def pair(index, carry):
        first = index * 4
        left, right = [], []
        for side in (0, 1):
            item = first + 2 * side
            left.append(split(jnp.where(lower, block(item, 0), block(item + 1, 1))))
            for slot in (0, 1):
                kind = kind_ref[item + slot] * 2 + side
                right.append((pattern_high[kind], pattern_low[kind]))
        left = [jnp.concatenate([part[half] for part in left], 1) for half in (0, 1)]
        right = [jnp.concatenate([part[half] for part in right], 0) for half in (0, 1)]
        out_ref[:, pl.ds(pl.multiple_of(index * LANES, LANES), LANES)] = dot3(left, right)
        return carry

    lax.fori_loop(0, out_ref.shape[1] // LANES, pair, 0, unroll=2)


def padded_patterns(patterns):
    zeros = jnp.zeros_like(patterns)
    left = jnp.concatenate([patterns, zeros], 2)
    right = jnp.concatenate([zeros, patterns], 2)
    return jnp.stack([left, right], 1).reshape(-1, BLK, LANES)


def beta_tables(me, own_count, links, kinds, coefs):
    links, kinds, coefs = [
        lax.dynamic_slice_in_dim(array, me * own_count, own_count, 0).reshape(-1)
        for array in (links, kinds, coefs)
    ]
    owner, place = lax.div(links, own_count), lax.rem(links, own_count)
    return owner, lax.div(place, 2), lax.rem(place, 2), kinds, coefs


def beta_term(me, device_count, layout, parts, tables, sides, shape):
    rows, cols = shape
    smem = pl.BlockSpec(memory_space=pltpu.SMEM)
    vmem = pl.BlockSpec(memory_space=pltpu.VMEM)
    return pl.pallas_call(
        functools.partial(beta_kernel, layout),
        in_specs=[smem] * 6 + [vmem] + [pl.BlockSpec(memory_space=pl.ANY)] * len(parts),
        out_specs=vmem,
        out_shape=jax.ShapeDtypeStruct(shape, jnp.float32),
        scratch_shapes=[
            pltpu.VMEM((device_count, rows, cols), jnp.float32),
            pltpu.VMEM(sides.shape, jnp.bfloat16),
            pltpu.VMEM(sides.shape, jnp.bfloat16),
            pltpu.SemaphoreType.DMA((len(parts),)),
        ],
        compiler_params=pltpu.CompilerParams(vmem_limit_bytes=40 * 2**20),
        cost_estimate=pl.CostEstimate(
            flops=12 * rows * cols * 4 * BLK,
            bytes_accessed=4 * rows * cols * (device_count + 1),
            transcendentals=0,
        ),
    )(me.reshape(1), *tables, sides, *parts)


def on_device(
    alpha_devices,
    beta_devices,
    ci_vector,
    patterns,
    alpha_links,
    alpha_kinds,
    alpha_coefs,
    beta_links,
    beta_kinds,
    beta_coefs,
):
    rows, cols = ci_vector.shape
    layers = alpha_devices // 2
    me = lax.axis_index("alpha")
    me_beta = lax.axis_index("beta")

    def over_alpha(value, flip):
        return lax.ppermute(value, "alpha", [(i, i ^ flip) for i in range(alpha_devices)])

    def over_beta(value, flip):
        return lax.ppermute(value, "beta", [(i, i ^ flip) for i in range(beta_devices)])

    plans = [
        ([2 * m for m in range(1, layers // 2)], layers),
        ([4 * m for m in range(1, layers // 2)], 2),
    ]
    width = cols // 4

    def start_of(kind, chunk):
        return (2 * kind + chunk) * width

    peer = over_alpha(ci_vector, 1)
    blocks = rows // BLK
    inner = jnp.arange(blocks, dtype=jnp.int32)
    targets, sources = [], []
    for members, partner in plans:
        flips = [0, 1] + [flip ^ core for flip in members for core in (0, 1)]
        targets.append(
            jnp.concatenate([(me ^ flip) * blocks + inner for flip in (0, partner)])
        )
        sources.append(jnp.concatenate([(me ^ flip) * blocks + inner for flip in flips]))
    sides = after(padded_patterns(patterns), peer)
    matrices = coupling_matrices(
        sides, alpha_links, alpha_kinds, alpha_coefs, jnp.stack(targets), jnp.stack(sources)
    )
    tables = beta_tables(me_beta, cols // BLK, beta_links, beta_kinds, beta_coefs)

    arrived = {}
    pieces = take(
        [ci_vector], [(0, 0, start_of(kind, 0)) for kind in (1, 0)], [(rows, width)] * 2, 56
    )
    pieces += take(
        [after(ci_vector, *matrices)],
        [(0, 0, start_of(kind, 1)) for kind in (1, 0)],
        [(rows, width)] * 2,
    )
    for chunk in (0, 1):
        for kind in (1, 0):
            piece = pieces[2 * chunk + 1 - kind]
            arrived[kind, chunk] = [over_alpha(piece, flip) for flip in plans[kind][0]]

    def swap(chunk, *earlier):
        swapped = []
        for kind in (0, 1):
            swapped.append([])
            for piece in arrived[kind, chunk]:
                swapped[kind] += [piece, over_alpha(after(piece, *earlier), 1)]
        return swapped

    own, others = {}, {}

    def multiply(chunk, swapped):
        sends = []
        for kind, (_, partner) in enumerate(plans):
            own[kind, chunk], send = alpha_products(
                kind, matrices, [ci_vector, peer], swapped[kind], start_of(kind, chunk), width
            )
            others[kind, chunk] = over_alpha(send, partner)
            sends.append(send)
        return sends

    sends = multiply(0, swap(0, *matrices, *tables, *pieces[2:]))

    whole = after(ci_vector, peer)
    gathered = {0: ci_vector}
    layout, parts = [(0, 0, rows)], [ci_vector]
    for flip in range(1, beta_devices):
        if flip & -flip == flip:
            gathered[flip] = over_beta(whole, flip)
            layout.append((flip, 0, rows))
            parts.append(gathered[flip])
    for flip in range(1, beta_devices):
        low = flip & -flip
        if low != flip:
            first, second = take(
                [after(gathered[flip ^ low], *sends), gathered[low]],
                [(0, 0, 0), (1, rows // 2, 0)],
                [(rows // 2, cols)] * 2,
            )
            top = over_beta(first, low)
            bottom = over_beta(second, flip ^ low)
            gathered[flip] = jnp.concatenate([top, bottom], 0)
            layout += [(flip, 0, rows // 2), (flip, rows // 2, rows // 2)]
            parts += [top, bottom]

    multiply(1, swap(1, *sends))
    total = beta_term(
        me_beta, beta_devices, tuple(layout), parts, tables, sides, (rows, cols)
    )
    total = total + jnp.concatenate(
        [own[kind, chunk] for kind in (0, 1) for chunk in (0, 1)], 1
    )
    total = add_at(
        total,
        [after(others[kind, 0], total) for kind in (0, 1)],
        [start_of(kind, 0) for kind in (0, 1)],
    )
    starts = [start_of(kind, 1) for kind in (0, 1)]
    bases = [total[:, start : start + width] for start in starts]
    last = [after(others[kind, 1], *bases) for kind in (0, 1)]
    return add_last(total, bases, last, starts)


def solution(mesh):
    return jax.shard_map(
        functools.partial(on_device, mesh.shape["alpha"], mesh.shape["beta"]),
        mesh=mesh,
        in_specs=(P("alpha", "beta"), P(), P(), P(), P(), P(), P(), P()),
        out_specs=P("alpha", "beta"),
        check_vma=False,
    )
```
